1024 devices in a mesh: row: 16 (over y, x_lo), col: 64 (over x_hi, z, core).
Axes of the slice: x: 4 (x_hi: 2, x_lo: 2; x = x_hi * 2 + x_lo), y: 8, z: 16, core: 2. Of those that a mesh axis runs over, the one named last changes fastest.
Arguments:
- images: bfloat16 [8192, 1152], P(('row', 'col')), may hold values from -0.1796875 to 0.1796875
- texts: bfloat16 [8192, 1152], P(('row', 'col')), may hold values from -0.1796875 to 0.1796875
- log_temp: float32 [1], replicated, may hold values from 1.6 to 2.5
- bias: float32 [1], replicated, may hold values from -4 to -2.5
Outputs:
- image_grad: float32 [8192, 1152], P(('row', 'col'))
- text_grad: float32 [8192, 1152], P(('row', 'col'))
The draws below stay inside these ranges and needn't reach their ends.
All inputs are finite; a program needn't handle non-finite values.
Results may differ from the reference program's by a relative error of at most 0.0047.
Values may be sent and summed in bfloat16 or wider, within the bound.
No kernel may reach another device: no remote copies, remote signals or barrier semaphores. Data moves between devices by JAX's collectives and lax.ppermute only.
A program may use at most 32 MiB of HBM per device.

```python
import jax
import jax.numpy as jnp
from jax import lax

D = 1152
BATCH = 8192
BLOCK = 512


def block_scale(rng, dims, cuts, least, high):
    loudness, own = 1.0, jax.random.fold_in(rng, 6)
    for dim, blocks in cuts:
        steps = jnp.exp(jax.random.uniform(jax.random.fold_in(own, dim), (blocks,), jnp.float32, least / len(cuts), high / len(cuts)))
        loudness = loudness * jnp.repeat(steps, dims[dim] // blocks).reshape([-1 if axis == dim else 1 for axis in range(len(dims))])
    return loudness


def scatter_about(own_key, dims, width, limit, cuts=(), kind=jnp.bfloat16):
    array = jax.random.normal(own_key, dims, jnp.float32) * width
    if len(cuts) > 0:
        array = block_scale(own_key, dims, cuts, -0.22, 0.18) * array
    return jnp.clip(array, min=-limit, max=limit).astype(kind)


def setup_inputs(seed: int = 0) -> dict:
    splits = jax.random.split(jax.random.key(seed), 5)
    return {
        "images": scatter_about(splits[0], (BATCH, D), 0.03, 0.1796875, ((0, 1024),)),
        "texts": scatter_about(splits[1], (BATCH, D), 0.03, 0.1796875, ((0, 1024),)),
        "log_temp": jnp.clip(jax.random.uniform(splits[2], (1,), jnp.float32, 1.6, 2.5), 1.6, 2.5),
        "bias": jnp.clip(jax.random.uniform(splits[3], (1,), jnp.float32, -4.0, -2.5), -4.0, -2.5),
    }


def unit_rows(values):
    whole = values.astype(jnp.float32)
    inverse = lax.rsqrt(lax.optimization_barrier(jnp.sum(whole * whole, axis=1, keepdims=True)) + 1e-06)
    return (whole * inverse, inverse)

def back_norm(unit, inverse, grads):
    return inverse * (grads - unit * lax.optimization_barrier(jnp.sum(unit * grads, axis=1, keepdims=True)))

def reference(images, texts, log_temp, bias):
    img_unit, inv_img = unit_rows(images)
    txt_unit, inv_txt = unit_rows(texts)
    img_half = img_unit.astype(jnp.bfloat16)
    txt_half = txt_unit.astype(jnp.bfloat16)
    scale = jnp.exp(log_temp[0])
    shift = bias[0]
    total = images.shape[0]
    nblocks = total // BLOCK

    def step(carry, index):
        start = (index * BLOCK).astype(jnp.int32)
        block = lax.dynamic_slice_in_dim(img_half, start, BLOCK, 0)
        scores = lax.dot_general(block, txt_half, (((1,), (1,)), ((), ())), preferred_element_type=jnp.float32)
        logits = scale * scores + shift
        rows = start + jnp.arange(BLOCK, dtype=jnp.int32)[:, None]
        cols = jnp.arange(total, dtype=jnp.int32)[None, :]
        labels = (rows == cols).astype(jnp.float32)
        dlogit = (jax.nn.sigmoid(logits) - labels).astype(jnp.bfloat16)
        dimg = jnp.dot(dlogit, txt_half, preferred_element_type=jnp.float32)
        part = lax.dot_general(dlogit, block, (((0,), (0,)), ((), ())), preferred_element_type=jnp.float32)
        return (carry + part, dimg)
    dtxt, dimg = lax.scan(step, jnp.zeros((total, D), jnp.float32), jnp.arange(nblocks, dtype=jnp.int32))
    dimg = scale * dimg.reshape(total, D)
    dtxt = scale * dtxt
    return (back_norm(img_unit, inv_img, dimg), back_norm(txt_unit, inv_txt, dtxt))
```

```python
import jax
import jax.numpy as jnp
from jax import lax
from jax.sharding import Mesh, PartitionSpec as P

AXES = ("y", "xl", "xh", "z", "c")
SIZES = (8, 2, 2, 16, 2)
PLANE = ("c", "xh", "xl", "y")
LINE = "z"


def unit_rows(values):
    whole = values.astype(jnp.float32)
    inverse = lax.rsqrt(jnp.sum(whole * whole, axis=1, keepdims=True) + 1e-06)
    return (whole * inverse, inverse)


def back_norm(unit, inverse, grads):
    return inverse * (grads - unit * jnp.sum(unit * grads, axis=1, keepdims=True))


def local(images, texts, log_temp, bias):
    shard, width = images.shape
    plane = lax.axis_size(PLANE)
    line = lax.axis_size(LINE)
    img_unit, inv_img = unit_rows(images)
    txt_unit, inv_txt = unit_rows(texts)
    img_half = img_unit.astype(jnp.bfloat16)
    txt_half = txt_unit.astype(jnp.bfloat16)
    scale = jnp.exp(log_temp[0])
    shift = bias[0]
    txt_group = lax.all_to_all(
        jnp.broadcast_to(txt_half[None], (plane, shard, width)), PLANE, 0, 0
    ).reshape(plane * shard, width)
    img_group = lax.all_gather(img_half, LINE, axis=0, tiled=True)
    scores = lax.dot_general(
        img_group, txt_group, (((1,), (1,)), ((), ())), preferred_element_type=jnp.float32
    )
    logits = scale * scores + shift
    rows = jnp.arange(line * shard, dtype=jnp.int32)[:, None] - lax.axis_index(LINE) * shard
    cols = jnp.arange(plane * shard, dtype=jnp.int32)[None, :] - lax.axis_index(PLANE) * shard
    labels = ((rows == cols) & (cols >= 0) & (cols < shard)).astype(jnp.float32)
    dlogit = (jax.nn.sigmoid(logits) - labels).astype(jnp.bfloat16)
    dimg = lax.dot_general(
        dlogit, txt_group, (((1,), (0,)), ((), ())), preferred_element_type=jnp.float32
    ).astype(jnp.bfloat16)
    img_parts = lax.all_to_all(dimg.reshape(line, shard, width), LINE, 0, 0)
    dtxt = lax.dot_general(
        dlogit, img_group, (((0,), (0,)), ((), ())), preferred_element_type=jnp.float32
    ).astype(jnp.bfloat16)
    txt_parts = lax.all_to_all(dtxt.reshape(plane, shard, width), PLANE, 0, 0)
    img_share = jnp.sum(img_parts.astype(jnp.float32), axis=0)
    txt_share = jnp.sum(txt_parts.astype(jnp.float32), axis=0)
    image_grad = back_norm(img_unit, inv_img, scale * img_share)
    text_grad = back_norm(txt_unit, inv_txt, scale * txt_share)
    return (image_grad, text_grad)


def solution(mesh):
    fine = Mesh(mesh.devices.reshape(SIZES), AXES)
    split = P(AXES, None)
    return jax.shard_map(
        local, mesh=fine, in_specs=(split, split, P(), P()), out_specs=(split, split), check_vma=False
    )
```

```python
import functools

import jax
import jax.numpy as jnp
from jax import lax
from jax.experimental import pallas as pl
from jax.experimental.pallas import tpu as pltpu
from jax.sharding import Mesh, PartitionSpec as P

AXES = ("y", "xl", "xh", "z", "c")
SIZES = (8, 2, 2, 16, 2)
RING = ("xh", "xl")
PLANE = ("xh", "xl", "y")
LINE = "z"

VMEM = pl.BlockSpec(memory_space=pltpu.VMEM)
SMEM = pl.BlockSpec(memory_space=pltpu.SMEM)


def unit_rows(values):
    whole = values.astype(jnp.float32)
    inverse = lax.rsqrt(jnp.sum(whole * whole, axis=1, keepdims=True) + 1e-06)
    return (whole * inverse, inverse)


def back_norm(unit, inverse, grads):
    return inverse * (grads - unit * jnp.sum(unit * grads, axis=1, keepdims=True))


def pairs_kernel(shard, place, knobs, img, txt, dimg, keep, send, dtxt):
    line, core, peer = place[0], place[1], place[2]
    scores = lax.dot_general(
        img[...], txt[...], (((1,), (1,)), ((), ())), preferred_element_type=jnp.float32
    )
    logits = knobs[0] * scores + knobs[1]
    rows = lax.broadcasted_iota(jnp.int32, logits.shape, 0) - line * shard
    cols = lax.broadcasted_iota(jnp.int32, logits.shape, 1) - (2 * peer + core) * shard
    same = (rows == cols) & (cols >= 0) & (cols < shard)
    dlogit = (jax.nn.sigmoid(logits) - same.astype(jnp.float32)).astype(jnp.bfloat16)
    dimg[...] = jnp.dot(dlogit, txt[...], preferred_element_type=jnp.float32).astype(jnp.bfloat16)
    dtxt[...] = lax.dot_general(
        dlogit, img[...], (((0,), (0,)), ((), ())), preferred_element_type=jnp.float32
    )
    for k in range(keep.shape[0] // shard):
        mine = pl.multiple_of((2 * k + core) * shard, shard)
        other = pl.multiple_of((2 * k + 1 - core) * shard, shard)
        keep[k * shard : (k + 1) * shard, :] = dtxt[pl.ds(mine, shard), :]
        send[k * shard : (k + 1) * shard, :] = dtxt[pl.ds(other, shard), :]


def pairs(shard, place, knobs, img, txt):
    width, half = img.shape[1], txt.shape[0] // 2
    return pl.pallas_call(
        functools.partial(pairs_kernel, shard),
        out_shape=(
            jax.ShapeDtypeStruct(img.shape, jnp.bfloat16),
            jax.ShapeDtypeStruct((half, width), jnp.float32),
            jax.ShapeDtypeStruct((half, width), jnp.float32),
        ),
        in_specs=[SMEM, SMEM, VMEM, VMEM],
        out_specs=(VMEM, VMEM, VMEM),
        scratch_shapes=[pltpu.VMEM(txt.shape, jnp.float32)],
        compiler_params=pltpu.CompilerParams(vmem_limit_bytes=24 << 20),
        cost_estimate=pl.CostEstimate(
            flops=6 * img.size * txt.shape[0], bytes_accessed=5 << 20, transcendentals=img.shape[0] * txt.shape[0]
        ),
    )(place, knobs, img, txt)


def split_kernel(place, keep, got, own, first, second, third):
    rows = own.shape[0]
    for step, out in enumerate((own, first, second, third)):
        part = pl.ds(pl.multiple_of(lax.rem(place[3] + step, 4) * rows, rows), rows)
        out[...] = (keep[part, :] + got[part, :]).astype(out.dtype)


def split(place, keep, got):
    part = (keep.shape[0] // 4, keep.shape[1])
    sent = jax.ShapeDtypeStruct(part, jnp.bfloat16)
    return pl.pallas_call(
        split_kernel,
        out_shape=(jax.ShapeDtypeStruct(part, jnp.float32), sent, sent, sent),
        in_specs=[SMEM, VMEM, VMEM],
        out_specs=(VMEM, VMEM, VMEM, VMEM),
        compiler_params=pltpu.CompilerParams(vmem_limit_bytes=16 << 20),
        cost_estimate=pl.CostEstimate(flops=keep.size, bytes_accessed=3 << 20, transcendentals=0),
    )(place, keep, got)


def at(x):
    return x % 2 * 2 + x // 2


def local(images, texts, log_temp, bias):
    shard, width = images.shape
    line, plane = lax.axis_size(LINE), lax.axis_size(PLANE)
    place = jnp.stack(
        [lax.axis_index(LINE), lax.axis_index("c"), lax.axis_index(PLANE), lax.axis_index(RING)]
    ).astype(jnp.int32)
    scale = jnp.exp(log_temp[0])
    knobs = jnp.stack([scale, bias[0]])
    img_unit, inv_img = unit_rows(images)
    txt_unit, inv_txt = unit_rows(texts)
    chip_half = unit_rows(lax.all_gather(texts, "c", axis=0, tiled=True))[0].astype(jnp.bfloat16)
    txt_group = lax.all_to_all(
        jnp.broadcast_to(chip_half[None], (plane, 2 * shard, width)), PLANE, 0, 0
    ).reshape(plane * 2 * shard, width)
    img_group = lax.all_gather(img_unit.astype(jnp.bfloat16), LINE, axis=0, tiled=True)
    dimg, keep, send = pairs(shard, place, knobs, img_group, txt_group)
    got = lax.ppermute(send, "c", [(0, 1), (1, 0)])
    img_parts = lax.all_to_all(dimg.reshape(line, shard, width), LINE, 0, 0)
    own, *parts = split(place, keep, got)
    for step, part in enumerate(parts, 1):
        moved = lax.ppermute(part, ("xl", "xh"), [(at(x), at((x + step) % 4)) for x in range(4)])
        own = own + moved.astype(jnp.float32)
    txt_parts = lax.all_to_all(own.astype(jnp.bfloat16).reshape(-1, shard, width), "y", 0, 0)
    img_share = jnp.sum(img_parts.astype(jnp.float32), axis=0)
    txt_share = jnp.sum(txt_parts.astype(jnp.float32), axis=0)
    image_grad = back_norm(img_unit, inv_img, scale * img_share)
    text_grad = back_norm(txt_unit, inv_txt, scale * txt_share)
    return (image_grad, text_grad)


def solution(mesh):
    fine = Mesh(mesh.devices.reshape(SIZES), AXES)
    rows = P(AXES, None)
    return jax.shard_map(
        local, mesh=fine, in_specs=(rows, rows, P(), P()), out_specs=(rows, rows), check_vma=False
    )
```

```python
import itertools

import jax
import jax.numpy as jnp
from jax import lax
from jax.experimental import pallas as pl
from jax.experimental.pallas import tpu as pltpu
from jax.sharding import Mesh, PartitionSpec as P

AXES = ("y", "xl", "xh", "z", "c")
SIZES = (8, 2, 2, 16, 2)

GROUP = 16

ROUND = [(1, 0), (0, 3), (3, 2), (2, 1)]
BACK = [(b, a) for a, b in ROUND]

VMEM = pl.BlockSpec(memory_space=pltpu.VMEM)
SMEM = pl.BlockSpec(memory_space=pltpu.SMEM)


def groups():
    place = {at: n for n, at in enumerate(itertools.product(*map(range, SIZES)))}
    y, xl, xh, z, _ = map(range, SIZES)
    lines = [[place[b, i, j, k, 1] for k in z] for b in y for i in xl for j in xh]
    planes = [[place[b, i, j, k, 0] for b in y for j in xh] for i in xl for k in z]
    return lines + planes


def unit_rows(values):
    whole = values.astype(jnp.float32)
    inverse = lax.rsqrt(jnp.sum(whole * whole, axis=1, keepdims=True) + 1e-06)
    return (whole * inverse, inverse)


def back_norm(unit, inverse, grads):
    return inverse * (grads - unit * jnp.sum(unit * grads, axis=1, keepdims=True))


def unit_kernel(chip, out):
    rows = out.shape[0] // GROUP
    shard = rows // 2
    whole = chip[...].astype(jnp.float32)
    images = jnp.concatenate([whole[:shard], whole[2 * shard : 3 * shard]])
    texts = jnp.concatenate([whole[shard : 2 * shard], whole[3 * shard :]])
    half = unit_rows(jnp.where(lax.axis_index("c") == 1, images, texts))[0].astype(jnp.bfloat16)
    for k in range(GROUP):
        out[k * rows : (k + 1) * rows, :] = half


def units(chip):
    return pl.pallas_call(
        unit_kernel,
        out_shape=jax.ShapeDtypeStruct((GROUP * chip.shape[0] // 2, chip.shape[1]), jnp.bfloat16),
        in_specs=[VMEM],
        out_specs=VMEM,
        compiler_params=pltpu.CompilerParams(vmem_limit_bytes=8 << 20),
        cost_estimate=pl.CostEstimate(flops=4 * chip.size, bytes_accessed=1 << 20, transcendentals=0),
    )(chip)


def pairs_kernel(log_temp, bias, mine, got, grad_mine, grad_got):
    rows, cols = mine.shape[0], got.shape[0]
    block = rows // GROUP
    scores = lax.dot_general(
        mine[...], got[...], (((1,), (1,)), ((), ())), preferred_element_type=jnp.float32
    )
    logits = jnp.exp(jnp.full((1, cols), log_temp[0], jnp.float32)) * scores + bias[0]
    row = lax.broadcasted_iota(jnp.int32, (rows, cols), 0)
    row = row - (lax.axis_index("y") * SIZES[2] + lax.axis_index("xh")) * block
    col = lax.broadcasted_iota(jnp.int32, (rows, cols), 1) - lax.axis_index("z") * block
    same = (row == col) & (row >= 0) & (row < block) & (lax.axis_index("c") == 0)
    dlogit = (jax.nn.sigmoid(logits) - jnp.where(same, 1.0, 0.0)).astype(jnp.bfloat16)
    grad_got[...] = lax.dot_general(
        dlogit, mine[...], (((0,), (0,)), ((), ())), preferred_element_type=jnp.float32
    ).astype(jnp.bfloat16)
    grad_mine[...] = jnp.dot(dlogit, got[...], preferred_element_type=jnp.float32)


def pairs(log_temp, bias, mine, got):
    return pl.pallas_call(
        pairs_kernel,
        out_shape=(
            jax.ShapeDtypeStruct(mine.shape, jnp.float32),
            jax.ShapeDtypeStruct(got.shape, jnp.bfloat16),
        ),
        in_specs=[SMEM, SMEM, VMEM, VMEM],
        out_specs=(VMEM, VMEM),
        compiler_params=pltpu.CompilerParams(vmem_limit_bytes=16 << 20),
        cost_estimate=pl.CostEstimate(
            flops=6 * mine.size * got.shape[0],
            bytes_accessed=3 << 20,
            transcendentals=mine.shape[0] * got.shape[0],
        ),
    )(log_temp, bias, mine, got)


def end_kernel(log_temp, sums, images, texts, image_grad, text_grad):
    shard, width = images.shape
    scale = jnp.exp(jnp.full((1, width), log_temp[0], jnp.float32))
    first = pl.multiple_of(lax.axis_index("c") * shard, shard)
    text_grad[...] = back_norm(*unit_rows(texts[...]), scale * sums[pl.ds(first, shard), :])
    image_grad[...] = back_norm(*unit_rows(images[...]), scale * sums[pl.ds(first + 2 * shard, shard), :])


def end(log_temp, sums, images, texts):
    grad = jax.ShapeDtypeStruct(images.shape, jnp.float32)
    return pl.pallas_call(
        end_kernel,
        out_shape=(grad, grad),
        in_specs=[SMEM, VMEM, VMEM, VMEM],
        out_specs=(VMEM, VMEM),
        compiler_params=pltpu.CompilerParams(vmem_limit_bytes=8 << 20),
        cost_estimate=pl.CostEstimate(flops=20 * images.size, bytes_accessed=1 << 18, transcendentals=0),
    )(log_temp, sums, images, texts)


def local(images, texts, log_temp, bias):
    width = images.shape[1]
    swap = groups()

    def exchange(rows):
        parts = rows.reshape(GROUP, -1, width)
        return lax.all_to_all(parts, AXES, 0, 0, axis_index_groups=swap)

    chip = lax.all_gather(jnp.concatenate([images, texts]), "c", axis=0, tiled=True)
    mine = exchange(units(chip)).reshape(-1, width)
    got = lax.ppermute(mine, ("xl", "c"), ROUND)
    grad_mine, grad_got = pairs(log_temp, bias, mine, got)
    total = grad_mine + lax.ppermute(grad_got, ("xl", "c"), BACK).astype(jnp.float32)
    share = jnp.sum(exchange(total.astype(jnp.bfloat16)).astype(jnp.float32), axis=0)
    sums = lax.all_gather(share, "c", axis=0, tiled=True)
    return end(log_temp, sums, images, texts)


def solution(mesh):
    fine = Mesh(mesh.devices.reshape(SIZES), AXES)
    rows = P(AXES, None)
    return jax.shard_map(
        local, mesh=fine, in_specs=(rows, rows, P(), P()), out_specs=(rows, rows), check_vma=False
    )
```

```python
import itertools

import jax
import jax.numpy as jnp
from jax import lax
from jax.experimental import pallas as pl
from jax.experimental.pallas import tpu as pltpu
from jax.sharding import Mesh, PartitionSpec as P

AXES = ("y", "xl", "xh", "z", "c")
SIZES = (8, 2, 2, 16, 2)

GROUP = 16

NEAR = ("xl", "xh", "c")


def moves(step):
    at = lambda x, c: x % 2 * 4 + x // 2 * 2 + c
    return [(at(x, c), at((x + step) % 4, 1 - c)) for x in range(4) for c in range(2)]


VMEM = pl.BlockSpec(memory_space=pltpu.VMEM)
SMEM = pl.BlockSpec(memory_space=pltpu.SMEM)


def groups():
    place = {at: n for n, at in enumerate(itertools.product(*map(range, SIZES)))}
    y, xl, xh, z, _ = map(range, SIZES)
    lines = [[place[b, i, j, k, 1] for k in z] for b in y for i in xl for j in xh]
    planes = [[place[b, i, j, k, 0] for b in y for j in xh] for i in xl for k in z]
    return lines + planes


def unit_rows(values):
    whole = values.astype(jnp.float32)
    inverse = lax.rsqrt(jnp.sum(whole * whole, axis=1, keepdims=True) + 1e-06)
    return (whole * inverse, inverse)


def back_norm(unit, inverse, grads):
    return inverse * (grads - unit * jnp.sum(unit * grads, axis=1, keepdims=True))


def unit_kernel(chip, out):
    rows = out.shape[0] // GROUP
    shard = rows // 2
    whole = chip[...].astype(jnp.float32)
    images = jnp.concatenate([whole[:shard], whole[2 * shard : 3 * shard]])
    texts = jnp.concatenate([whole[shard : 2 * shard], whole[3 * shard :]])
    half = unit_rows(jnp.where(lax.axis_index("c") == 1, images, texts))[0].astype(jnp.bfloat16)
    for k in range(GROUP):
        out[k * rows : (k + 1) * rows, :] = half


def units(chip):
    return pl.pallas_call(
        unit_kernel,
        out_shape=jax.ShapeDtypeStruct((GROUP * chip.shape[0] // 2, chip.shape[1]), jnp.bfloat16),
        in_specs=[VMEM],
        out_specs=VMEM,
        compiler_params=pltpu.CompilerParams(vmem_limit_bytes=8 << 20),
        cost_estimate=pl.CostEstimate(flops=4 * chip.size, bytes_accessed=1 << 20, transcendentals=0),
    )(chip)


def pairs_kernel(log_temp, bias, mine, own, before, after, grad):
    block = mine.shape[0] // GROUP
    line = lax.axis_index("z") * block
    plane = (lax.axis_index("y") * SIZES[2] + lax.axis_index("xh")) * block
    image = lax.axis_index("c") == 1
    total = jnp.zeros(mine.shape, jnp.float32)
    for got in (own, before, after):
        scores = lax.dot_general(
            mine[...], got[...], (((1,), (1,)), ((), ())), preferred_element_type=jnp.float32
        )
        logits = jnp.exp(jnp.full((1, got.shape[0]), log_temp[0], jnp.float32)) * scores + bias[0]
        slope = jax.nn.sigmoid(logits)
        if got is own:
            row = lax.broadcasted_iota(jnp.int32, slope.shape, 0) - jnp.where(image, line, plane)
            col = lax.broadcasted_iota(jnp.int32, slope.shape, 1) - jnp.where(image, plane, line)
            same = (row == col) & (row >= 0) & (row < block)
            slope = slope - jnp.where(same, 1.0, 0.0)
        total = total + jnp.dot(slope.astype(jnp.bfloat16), got[...], preferred_element_type=jnp.float32)
    grad[...] = total.astype(jnp.bfloat16)


def pairs(log_temp, bias, mine, own, before, after):
    others = own.shape[0] + before.shape[0] + after.shape[0]
    return pl.pallas_call(
        pairs_kernel,
        out_shape=jax.ShapeDtypeStruct(mine.shape, jnp.bfloat16),
        in_specs=[SMEM, SMEM, VMEM, VMEM, VMEM, VMEM],
        out_specs=VMEM,
        compiler_params=pltpu.CompilerParams(vmem_limit_bytes=24 << 20),
        cost_estimate=pl.CostEstimate(
            flops=4 * mine.size * others, bytes_accessed=3 << 20, transcendentals=mine.shape[0] * others
        ),
    )(log_temp, bias, mine, own, before, after)


def end_kernel(log_temp, sums, images, texts, image_grad, text_grad):
    shard, width = images.shape
    scale = jnp.exp(jnp.full((1, width), log_temp[0], jnp.float32))
    first = pl.multiple_of(lax.axis_index("c") * shard, shard)
    text_grad[...] = back_norm(*unit_rows(texts[...]), scale * sums[pl.ds(first, shard), :])
    image_grad[...] = back_norm(*unit_rows(images[...]), scale * sums[pl.ds(first + 2 * shard, shard), :])


def end(log_temp, sums, images, texts):
    grad = jax.ShapeDtypeStruct(images.shape, jnp.float32)
    return pl.pallas_call(
        end_kernel,
        out_shape=(grad, grad),
        in_specs=[SMEM, VMEM, VMEM, VMEM],
        out_specs=(VMEM, VMEM),
        compiler_params=pltpu.CompilerParams(vmem_limit_bytes=8 << 20),
        cost_estimate=pl.CostEstimate(flops=20 * images.size, bytes_accessed=1 << 18, transcendentals=0),
    )(log_temp, sums, images, texts)


def local(images, texts, log_temp, bias):
    width = images.shape[1]
    swap = groups()

    def exchange(rows):
        parts = rows.reshape(GROUP, -1, width)
        return lax.all_to_all(parts, AXES, 0, 0, axis_index_groups=swap)

    chip = lax.all_gather(jnp.concatenate([images, texts]), "c", axis=0, tiled=True)
    mine = exchange(units(chip)).reshape(-1, width)
    half = mine.shape[0] // 2
    before = lax.ppermute(mine[:half], NEAR, moves(1))
    after = lax.ppermute(mine[half:], NEAR, moves(-1))
    own = lax.ppermute(mine, NEAR, moves(0))
    grad = pairs(log_temp, bias, mine, own, before, after)
    share = jnp.sum(exchange(grad).astype(jnp.float32), axis=0)
    sums = lax.all_gather(share, "c", axis=0, tiled=True)
    return end(log_temp, sums, images, texts)


def solution(mesh):
    fine = Mesh(mesh.devices.reshape(SIZES), AXES)
    rows = P(AXES, None)
    return jax.shard_map(
        local, mesh=fine, in_specs=(rows, rows, P(), P()), out_specs=(rows, rows), check_vma=False
    )
```

```python
import itertools

import jax
import jax.numpy as jnp
from jax import lax
from jax.experimental import pallas as pl
from jax.experimental.pallas import tpu as pltpu
from jax.sharding import Mesh, PartitionSpec as P

AXES = ("y", "xl", "xh", "z", "c")
SIZES = (8, 2, 2, 16, 2)

GROUP = 16

NEAR = ("xl", "xh", "c")


def moves(step):
    at = lambda x, c: x % 2 * 4 + x // 2 * 2 + c
    return [(at(x, c), at((x + step) % 4, 1 - c)) for x in range(4) for c in range(2)]


VMEM = pl.BlockSpec(memory_space=pltpu.VMEM)
SMEM = pl.BlockSpec(memory_space=pltpu.SMEM)


def groups():
    place = {at: n for n, at in enumerate(itertools.product(*map(range, SIZES)))}
    y, xl, xh, z, _ = map(range, SIZES)
    lines = [[place[b, i, j, k, 1] for k in z] for b in y for i in xl for j in xh]
    planes = [[place[b, i, j, k, 0] for j in xh for b in (y if j == 0 else y[::-1])] for i in xl for k in z]
    return lines + planes


def unit_rows(values):
    whole = values.astype(jnp.float32)
    inverse = lax.rsqrt(jnp.sum(whole * whole, axis=1, keepdims=True) + 1e-06)
    return (whole * inverse, inverse)


def back_norm(unit, inverse, grads):
    return inverse * (grads - unit * jnp.sum(unit * grads, axis=1, keepdims=True))


def unit_kernel(chip, out):
    shard = chip.shape[0] // 4
    whole = chip[...].astype(jnp.float32)
    images = jnp.concatenate([whole[:shard], whole[2 * shard : 3 * shard]])
    texts = jnp.concatenate([whole[shard : 2 * shard], whole[3 * shard :]])
    out[...] = unit_rows(jnp.where(lax.axis_index("c") == 1, images, texts))[0].astype(jnp.bfloat16)


def units(chip):
    return pl.pallas_call(
        unit_kernel,
        out_shape=jax.ShapeDtypeStruct((chip.shape[0] // 2, chip.shape[1]), jnp.bfloat16),
        in_specs=[VMEM],
        out_specs=VMEM,
        compiler_params=pltpu.CompilerParams(vmem_limit_bytes=8 << 20),
        cost_estimate=pl.CostEstimate(flops=4 * chip.size, bytes_accessed=1 << 20, transcendentals=0),
    )(chip)


def pairs_kernel(log_temp, bias, mine, own, before, after, grad):
    block = mine.shape[0] // GROUP
    line = lax.axis_index("z") * block
    y = lax.axis_index("y")
    plane = jnp.where(lax.axis_index("xh") == 0, y, GROUP - 1 - y) * block
    image = lax.axis_index("c") == 1
    total = jnp.zeros(mine.shape, jnp.float32)
    for got in (own, before, after):
        scores = lax.dot_general(
            mine[...], got[...], (((1,), (1,)), ((), ())), preferred_element_type=jnp.float32
        )
        logits = jnp.exp(jnp.full((1, got.shape[0]), log_temp[0], jnp.float32)) * scores + bias[0]
        slope = jax.nn.sigmoid(logits)
        if got is own:
            row = lax.broadcasted_iota(jnp.int32, slope.shape, 0) - jnp.where(image, line, plane)
            col = lax.broadcasted_iota(jnp.int32, slope.shape, 1) - jnp.where(image, plane, line)
            same = (row == col) & (row >= 0) & (row < block)
            slope = slope - jnp.where(same, 1.0, 0.0)
        total = total + jnp.dot(slope.astype(jnp.bfloat16), got[...], preferred_element_type=jnp.float32)
    grad[...] = total.astype(jnp.bfloat16)


def pairs(log_temp, bias, mine, own, before, after):
    others = own.shape[0] + before.shape[0] + after.shape[0]
    return pl.pallas_call(
        pairs_kernel,
        out_shape=jax.ShapeDtypeStruct(mine.shape, jnp.bfloat16),
        in_specs=[SMEM, SMEM, VMEM, VMEM, VMEM, VMEM],
        out_specs=VMEM,
        compiler_params=pltpu.CompilerParams(vmem_limit_bytes=24 << 20),
        cost_estimate=pl.CostEstimate(
            flops=4 * mine.size * others, bytes_accessed=3 << 20, transcendentals=mine.shape[0] * others
        ),
    )(log_temp, bias, mine, own, before, after)


def end_kernel(log_temp, sums, images, texts, image_grad, text_grad):
    shard, width = images.shape
    scale = jnp.exp(jnp.full((1, width), log_temp[0], jnp.float32))
    first = pl.multiple_of(lax.axis_index("c") * shard, shard)
    text_grad[...] = back_norm(*unit_rows(texts[...]), scale * sums[pl.ds(first, shard), :])
    image_grad[...] = back_norm(*unit_rows(images[...]), scale * sums[pl.ds(first + 2 * shard, shard), :])


def end(log_temp, sums, images, texts):
    grad = jax.ShapeDtypeStruct(images.shape, jnp.float32)
    return pl.pallas_call(
        end_kernel,
        out_shape=(grad, grad),
        in_specs=[SMEM, VMEM, VMEM, VMEM],
        out_specs=(VMEM, VMEM),
        compiler_params=pltpu.CompilerParams(vmem_limit_bytes=8 << 20),
        cost_estimate=pl.CostEstimate(flops=20 * images.size, bytes_accessed=1 << 18, transcendentals=0),
    )(log_temp, sums, images, texts)


def local(images, texts, log_temp, bias):
    width = images.shape[1]
    swap = groups()

    def exchange(rows):
        parts = rows.reshape(GROUP, -1, width)
        return lax.all_to_all(parts, AXES, 0, 0, axis_index_groups=swap)

    chip = lax.all_gather(jnp.concatenate([images, texts]), "c", axis=0, tiled=True)
    mine = lax.all_gather(units(chip), AXES, axis=0, tiled=True, axis_index_groups=swap)
    half = mine.shape[0] // 2
    before = lax.ppermute(mine[:half], NEAR, moves(1))
    after = lax.ppermute(mine[half:], NEAR, moves(-1))
    own = lax.ppermute(mine, NEAR, moves(0))
    grad = pairs(log_temp, bias, mine, own, before, after)
    share = jnp.sum(exchange(grad).astype(jnp.float32), axis=0)
    sums = lax.all_gather(share, "c", axis=0, tiled=True)
    return end(log_temp, sums, images, texts)


def solution(mesh):
    fine = Mesh(mesh.devices.reshape(SIZES), AXES)
    rows = P(AXES, None)
    return jax.shard_map(
        local, mesh=fine, in_specs=(rows, rows, P(), P()), out_specs=(rows, rows), check_vma=False
    )
```

```python
import itertools

import jax
import jax.numpy as jnp
from jax import lax
from jax.experimental import pallas as pl
from jax.experimental.pallas import tpu as pltpu
from jax.sharding import Mesh, PartitionSpec as P

AXES = ("y", "xl", "xh", "z", "c")
SIZES = (8, 2, 2, 16, 2)

GROUP = 16

NEAR = ("xl", "xh", "c")


def moves(step):
    at = lambda x, c: x % 2 * 4 + x // 2 * 2 + c
    return [(at(x, c), at((x + step) % 4, 1 - c)) for x in range(4) for c in range(2)]


VMEM = pl.BlockSpec(memory_space=pltpu.VMEM)
SMEM = pl.BlockSpec(memory_space=pltpu.SMEM)


def groups():
    place = {at: n for n, at in enumerate(itertools.product(*map(range, SIZES)))}
    y, xl, xh, z, _ = map(range, SIZES)
    lines = [[place[b, i, j, k, 1] for k in z] for b in y for i in xl for j in xh]
    planes = [[place[b, i, j, k, 0] for b in y for j in xh] for i in xl for k in z]
    return lines + planes


def unit_rows(values):
    whole = values.astype(jnp.float32)
    inverse = lax.rsqrt(jnp.sum(whole * whole, axis=1, keepdims=True) + 1e-06)
    return (whole * inverse, inverse)


def back_norm(unit, inverse, grads):
    return inverse * (grads - unit * jnp.sum(unit * grads, axis=1, keepdims=True))


def unit_kernel(chip, out):
    rows = out.shape[0] // GROUP
    shard = rows // 2
    whole = chip[...].astype(jnp.float32)
    images = jnp.concatenate([whole[:shard], whole[2 * shard : 3 * shard]])
    texts = jnp.concatenate([whole[shard : 2 * shard], whole[3 * shard :]])
    half = unit_rows(jnp.where(lax.axis_index("c") == 1, images, texts))[0].astype(jnp.bfloat16)
    for k in range(GROUP):
        out[k * rows : (k + 1) * rows, :] = half


def units(chip):
    return pl.pallas_call(
        unit_kernel,
        out_shape=jax.ShapeDtypeStruct((GROUP * chip.shape[0] // 2, chip.shape[1]), jnp.bfloat16),
        in_specs=[VMEM],
        out_specs=VMEM,
        compiler_params=pltpu.CompilerParams(vmem_limit_bytes=8 << 20),
        cost_estimate=pl.CostEstimate(flops=4 * chip.size, bytes_accessed=1 << 20, transcendentals=0),
    )(chip)


def pairs_kernel(log_temp, bias, mine, first, second, beside, grad):
    block = mine.shape[0] // GROUP
    line = lax.axis_index("z") * block
    plane = (lax.axis_index("y") * SIZES[2] + lax.axis_index("xh")) * block
    image = lax.axis_index("c") == 1
    total = jnp.zeros(mine.shape, jnp.float32)
    for got, start in ((first, 0), (second, first.shape[0]), (beside, None)):
        scores = lax.dot_general(
            mine[...], got[...], (((1,), (1,)), ((), ())), preferred_element_type=jnp.float32
        )
        logits = jnp.exp(jnp.full((1, got.shape[0]), log_temp[0], jnp.float32)) * scores + bias[0]
        slope = jax.nn.sigmoid(logits)
        if start is not None:
            row = lax.broadcasted_iota(jnp.int32, slope.shape, 0) - jnp.where(image, line, plane)
            col = lax.broadcasted_iota(jnp.int32, slope.shape, 1) + start - jnp.where(image, plane, line)
            same = (row == col) & (row >= 0) & (row < block)
            slope = slope - jnp.where(same, 1.0, 0.0)
        total = total + jnp.dot(slope.astype(jnp.bfloat16), got[...], preferred_element_type=jnp.float32)
    grad[...] = total.astype(jnp.bfloat16)


def pairs(log_temp, bias, mine, first, second, beside):
    others = first.shape[0] + second.shape[0] + beside.shape[0]
    return pl.pallas_call(
        pairs_kernel,
        out_shape=jax.ShapeDtypeStruct(mine.shape, jnp.bfloat16),
        in_specs=[SMEM, SMEM, VMEM, VMEM, VMEM, VMEM],
        out_specs=VMEM,
        compiler_params=pltpu.CompilerParams(vmem_limit_bytes=24 << 20),
        cost_estimate=pl.CostEstimate(
            flops=4 * mine.size * others, bytes_accessed=3 << 20, transcendentals=mine.shape[0] * others
        ),
    )(log_temp, bias, mine, first, second, beside)


def end_kernel(log_temp, sums, images, texts, image_grad, text_grad):
    shard, width = images.shape
    scale = jnp.exp(jnp.full((1, width), log_temp[0], jnp.float32))
    first = pl.multiple_of(lax.axis_index("c") * shard, shard)
    text_grad[...] = back_norm(*unit_rows(texts[...]), scale * sums[pl.ds(first, shard), :])
    image_grad[...] = back_norm(*unit_rows(images[...]), scale * sums[pl.ds(first + 2 * shard, shard), :])


def end(log_temp, sums, images, texts):
    grad = jax.ShapeDtypeStruct(images.shape, jnp.float32)
    return pl.pallas_call(
        end_kernel,
        out_shape=(grad, grad),
        in_specs=[SMEM, VMEM, VMEM, VMEM],
        out_specs=(VMEM, VMEM),
        compiler_params=pltpu.CompilerParams(vmem_limit_bytes=8 << 20),
        cost_estimate=pl.CostEstimate(flops=20 * images.size, bytes_accessed=1 << 18, transcendentals=0),
    )(log_temp, sums, images, texts)


def local(images, texts, log_temp, bias):
    width = images.shape[1]
    swap = groups()

    def exchange(rows):
        parts = rows.reshape(GROUP, -1, width)
        return lax.all_to_all(parts, AXES, 0, 0, axis_index_groups=swap)

    chip = lax.all_gather(jnp.concatenate([images, texts]), "c", axis=0, tiled=True)
    mine = exchange(units(chip)).reshape(-1, width)
    half = mine.shape[0] // 2
    before = lax.ppermute(mine[:half], NEAR, moves(1))
    after = lax.ppermute(mine[half:], NEAR, moves(-1))
    own = [lax.ppermute(part, NEAR, moves(0)) for part in (mine[:half], mine[half:])]
    grad = pairs(log_temp, bias, mine, *own, jnp.concatenate([before, after]))
    share = jnp.sum(exchange(grad).astype(jnp.float32), axis=0)
    sums = lax.all_gather(share, "c", axis=0, tiled=True)
    return end(log_temp, sums, images, texts)


def solution(mesh):
    fine = Mesh(mesh.devices.reshape(SIZES), AXES)
    rows = P(AXES, None)
    return jax.shard_map(
        local, mesh=fine, in_specs=(rows, rows, P(), P()), out_specs=(rows, rows), check_vma=False
    )
```

```python
import itertools

import jax
import jax.numpy as jnp
from jax import lax
from jax.experimental import pallas as pl
from jax.experimental.pallas import tpu as pltpu
from jax.sharding import Mesh, PartitionSpec as P

AXES = ("y", "xl", "xh", "z", "c")
SIZES = (8, 2, 2, 16, 2)

GROUP = 16

TURN = 7

NEAR = ("xl", "xh", "c")


def moves(step):
    at = lambda x, c: x % 2 * 4 + x // 2 * 2 + c
    return [(at(x, c), at((x + step) % 4, 1 - c)) for x in range(4) for c in range(2)]


VMEM = pl.BlockSpec(memory_space=pltpu.VMEM)
SMEM = pl.BlockSpec(memory_space=pltpu.SMEM)


def groups():
    place = {at: n for n, at in enumerate(itertools.product(*map(range, SIZES)))}
    y, xl, xh, z, _ = map(range, SIZES)
    lines = [[place[b, i, j, k * TURN % GROUP, 1] for k in z] for b in y for i in xl for j in xh]
    planes = [[place[b, i, j, k, 0] for b in y for j in xh] for i in xl for k in z]
    return lines + planes


def unit_rows(values):
    whole = values.astype(jnp.float32)
    inverse = lax.rsqrt(jnp.sum(whole * whole, axis=1, keepdims=True) + 1e-06)
    return (whole * inverse, inverse)


def back_norm(unit, inverse, grads):
    return inverse * (grads - unit * jnp.sum(unit * grads, axis=1, keepdims=True))


def unit_kernel(chip, out):
    rows = out.shape[0] // GROUP
    shard = rows // 2
    whole = chip[...].astype(jnp.float32)
    images = jnp.concatenate([whole[:shard], whole[2 * shard : 3 * shard]])
    texts = jnp.concatenate([whole[shard : 2 * shard], whole[3 * shard :]])
    half = unit_rows(jnp.where(lax.axis_index("c") == 1, images, texts))[0].astype(jnp.bfloat16)
    for k in range(GROUP):
        out[k * rows : (k + 1) * rows, :] = half


def units(chip):
    return pl.pallas_call(
        unit_kernel,
        out_shape=jax.ShapeDtypeStruct((GROUP * chip.shape[0] // 2, chip.shape[1]), jnp.bfloat16),
        in_specs=[VMEM],
        out_specs=VMEM,
        compiler_params=pltpu.CompilerParams(vmem_limit_bytes=8 << 20),
        cost_estimate=pl.CostEstimate(flops=4 * chip.size, bytes_accessed=1 << 20, transcendentals=0),
    )(chip)


def slopes(log_temp, bias, mine, got):
    scores = lax.dot_general(mine, got, (((1,), (1,)), ((), ())), preferred_element_type=jnp.float32)
    logits = jnp.exp(jnp.full((1, got.shape[0]), log_temp[0], jnp.float32)) * scores + bias[0]
    return jax.nn.sigmoid(logits)


def times(slope, got):
    return jnp.dot(slope.astype(jnp.bfloat16), got, preferred_element_type=jnp.float32)


def before_kernel(log_temp, bias, mine, got, total):
    total[...] = times(slopes(log_temp, bias, mine[...], got[...]), got[...])


def after_kernel(log_temp, bias, mine, got, above, total):
    total[...] = above[...] + times(slopes(log_temp, bias, mine[...], got[...]), got[...])


def chip_kernel(log_temp, bias, mine, first, second, above, grad):
    block = mine.shape[0] // GROUP
    line = lax.rem(lax.axis_index("z") * TURN, GROUP) * block
    plane = (lax.axis_index("y") * SIZES[2] + lax.axis_index("xh")) * block
    image = lax.axis_index("c") == 1
    total = above[...]
    for got, start in ((first, 0), (second, first.shape[0])):
        slope = slopes(log_temp, bias, mine[...], got[...])
        row = lax.broadcasted_iota(jnp.int32, slope.shape, 0) - jnp.where(image, line, plane)
        col = lax.broadcasted_iota(jnp.int32, slope.shape, 1) + start - jnp.where(image, plane, line)
        same = (row == col) & (row >= 0) & (row < block)
        total = total + times(slope - jnp.where(same, 1.0, 0.0), got[...])
    grad[...] = total.astype(jnp.bfloat16)


def pairs(kernel, kind, log_temp, bias, mine, *others):
    rows = sum(got.shape[0] for got in others if got.dtype == mine.dtype)
    return pl.pallas_call(
        kernel,
        out_shape=jax.ShapeDtypeStruct(mine.shape, kind),
        in_specs=[SMEM, SMEM] + [VMEM] * (1 + len(others)),
        out_specs=VMEM,
        compiler_params=pltpu.CompilerParams(vmem_limit_bytes=24 << 20),
        cost_estimate=pl.CostEstimate(
            flops=4 * mine.size * rows, bytes_accessed=4 << 20, transcendentals=mine.shape[0] * rows
        ),
    )(log_temp, bias, mine, *others)


def end_kernel(log_temp, sums, images, texts, image_grad, text_grad):
    shard, width = images.shape
    scale = jnp.exp(jnp.full((1, width), log_temp[0], jnp.float32))
    first = pl.multiple_of(lax.axis_index("c") * shard, shard)
    text_grad[...] = back_norm(*unit_rows(texts[...]), scale * sums[pl.ds(first, shard), :])
    image_grad[...] = back_norm(*unit_rows(images[...]), scale * sums[pl.ds(first + 2 * shard, shard), :])


def end(log_temp, sums, images, texts):
    grad = jax.ShapeDtypeStruct(images.shape, jnp.float32)
    return pl.pallas_call(
        end_kernel,
        out_shape=(grad, grad),
        in_specs=[SMEM, VMEM, VMEM, VMEM],
        out_specs=(VMEM, VMEM),
        compiler_params=pltpu.CompilerParams(vmem_limit_bytes=8 << 20),
        cost_estimate=pl.CostEstimate(flops=20 * images.size, bytes_accessed=1 << 18, transcendentals=0),
    )(log_temp, sums, images, texts)


def local(images, texts, log_temp, bias):
    width = images.shape[1]
    swap = groups()

    def exchange(rows):
        parts = rows.reshape(GROUP, -1, width)
        return lax.all_to_all(parts, AXES, 0, 0, axis_index_groups=swap)

    chip = lax.all_gather(jnp.concatenate([images, texts]), "c", axis=0, tiled=True)
    mine = exchange(units(chip)).reshape(-1, width)
    halves = jnp.split(mine, 2)
    before = lax.ppermute(halves[0], NEAR, moves(1))
    after = lax.ppermute(halves[1], NEAR, moves(-1))
    own = [lax.ppermute(half, NEAR, moves(0)) for half in halves]
    total = pairs(before_kernel, jnp.float32, log_temp, bias, mine, before)
    total = pairs(after_kernel, jnp.float32, log_temp, bias, mine, after, total)
    grad = pairs(chip_kernel, jnp.bfloat16, log_temp, bias, mine, *own, total)
    share = jnp.sum(exchange(grad).astype(jnp.float32), axis=0)
    sums = lax.all_gather(share, "c", axis=0, tiled=True)
    return end(log_temp, sums, images, texts)


def solution(mesh):
    fine = Mesh(mesh.devices.reshape(SIZES), AXES)
    rows = P(AXES, None)
    return jax.shard_map(
        local, mesh=fine, in_specs=(rows, rows, P(), P()), out_specs=(rows, rows), check_vma=False
    )
```

```python
import itertools

import jax
import jax.numpy as jnp
from jax import lax
from jax.experimental import pallas as pl
from jax.experimental.pallas import tpu as pltpu
from jax.sharding import Mesh, PartitionSpec as P

AXES = ("y", "xl", "xh", "z", "c")
SIZES = (8, 2, 2, 16, 2)

GROUP = 16

NEAR = ("xl", "xh", "c")


def moves(step):
    at = lambda x, c: x % 4 % 2 * 4 + x % 4 // 2 * 2 + c
    return [(at(x, c), at(x - step if c else x + step, 1 - c)) for x in range(4) for c in range(2)]


VMEM = pl.BlockSpec(memory_space=pltpu.VMEM)
SMEM = pl.BlockSpec(memory_space=pltpu.SMEM)


def groups():
    place = {at: n for n, at in enumerate(itertools.product(*map(range, SIZES)))}
    y, xl, xh, z, _ = map(range, SIZES)
    lines = [[place[b, i, j, k, 1] for k in z] for b in y for i in xl for j in xh]
    planes = [[place[b, i, j, k, 0] for b in y for j in xh] for i in xl for k in z]
    return lines + planes


def unit_rows(values):
    whole = values.astype(jnp.float32)
    inverse = lax.rsqrt(jnp.sum(whole * whole, axis=1, keepdims=True) + 1e-06)
    return (whole * inverse, inverse)


def back_norm(unit, inverse, grads):
    return inverse * (grads - unit * jnp.sum(unit * grads, axis=1, keepdims=True))


def unit_kernel(chip, out):
    rows = out.shape[0] // GROUP
    shard = rows // 2
    whole = chip[...].astype(jnp.float32)
    images = jnp.concatenate([whole[:shard], whole[2 * shard : 3 * shard]])
    texts = jnp.concatenate([whole[shard : 2 * shard], whole[3 * shard :]])
    half = unit_rows(jnp.where(lax.axis_index("c") == 1, images, texts))[0].astype(jnp.bfloat16)
    for k in range(GROUP):
        out[k * rows : (k + 1) * rows, :] = half


def units(chip):
    return pl.pallas_call(
        unit_kernel,
        out_shape=jax.ShapeDtypeStruct((GROUP * chip.shape[0] // 2, chip.shape[1]), jnp.bfloat16),
        in_specs=[VMEM],
        out_specs=VMEM,
        compiler_params=pltpu.CompilerParams(vmem_limit_bytes=8 << 20),
        cost_estimate=pl.CostEstimate(flops=4 * chip.size, bytes_accessed=1 << 20, transcendentals=0),
    )(chip)


def pairs_kernel(log_temp, bias, mine, first, second, beside, grad):
    block = mine.shape[0] // GROUP
    line = lax.axis_index("z") * block
    plane = (lax.axis_index("y") * SIZES[2] + lax.axis_index("xh")) * block
    image = lax.axis_index("c") == 1
    total = jnp.zeros(mine.shape, jnp.float32)
    for got, start in ((first, 0), (second, first.shape[0]), (beside, None)):
        scores = lax.dot_general(
            mine[...], got[...], (((1,), (1,)), ((), ())), preferred_element_type=jnp.float32
        )
        logits = jnp.exp(jnp.full((1, got.shape[0]), log_temp[0], jnp.float32)) * scores + bias[0]
        slope = jax.nn.sigmoid(logits)
        if start is not None:
            row = lax.broadcasted_iota(jnp.int32, slope.shape, 0) - jnp.where(image, line, plane)
            col = lax.broadcasted_iota(jnp.int32, slope.shape, 1) + start - jnp.where(image, plane, line)
            same = (row == col) & (row >= 0) & (row < block)
            slope = slope - jnp.where(same, 1.0, 0.0)
        total = total + jnp.dot(slope.astype(jnp.bfloat16), got[...], preferred_element_type=jnp.float32)
    grad[...] = total.astype(jnp.bfloat16)


def pairs(log_temp, bias, mine, first, second, beside):
    others = first.shape[0] + second.shape[0] + beside.shape[0]
    return pl.pallas_call(
        pairs_kernel,
        out_shape=jax.ShapeDtypeStruct(mine.shape, jnp.bfloat16),
        in_specs=[SMEM, SMEM, VMEM, VMEM, VMEM, VMEM],
        out_specs=VMEM,
        compiler_params=pltpu.CompilerParams(vmem_limit_bytes=24 << 20),
        cost_estimate=pl.CostEstimate(
            flops=4 * mine.size * others, bytes_accessed=3 << 20, transcendentals=mine.shape[0] * others
        ),
    )(log_temp, bias, mine, first, second, beside)


def end_kernel(log_temp, sums, images, texts, image_grad, text_grad):
    shard, width = images.shape
    scale = jnp.exp(jnp.full((1, width), log_temp[0], jnp.float32))
    first = pl.multiple_of(lax.axis_index("c") * shard, shard)
    text_grad[...] = back_norm(*unit_rows(texts[...]), scale * sums[pl.ds(first, shard), :])
    image_grad[...] = back_norm(*unit_rows(images[...]), scale * sums[pl.ds(first + 2 * shard, shard), :])


def end(log_temp, sums, images, texts):
    grad = jax.ShapeDtypeStruct(images.shape, jnp.float32)
    return pl.pallas_call(
        end_kernel,
        out_shape=(grad, grad),
        in_specs=[SMEM, VMEM, VMEM, VMEM],
        out_specs=(VMEM, VMEM),
        compiler_params=pltpu.CompilerParams(vmem_limit_bytes=8 << 20),
        cost_estimate=pl.CostEstimate(flops=20 * images.size, bytes_accessed=1 << 18, transcendentals=0),
    )(log_temp, sums, images, texts)


def local(images, texts, log_temp, bias):
    width = images.shape[1]
    swap = groups()

    def exchange(rows):
        parts = rows.reshape(GROUP, -1, width)
        return lax.all_to_all(parts, AXES, 0, 0, axis_index_groups=swap)

    chip = lax.all_gather(jnp.concatenate([images, texts]), "c", axis=0, tiled=True)
    mine = exchange(units(chip)).reshape(-1, width)
    beside = lax.ppermute(mine, NEAR, moves(1))
    own = [lax.ppermute(half, NEAR, moves(0)) for half in jnp.split(mine, 2)]
    grad = pairs(log_temp, bias, mine, *own, beside)
    share = jnp.sum(exchange(grad).astype(jnp.float32), axis=0)
    sums = lax.all_gather(share, "c", axis=0, tiled=True)
    return end(log_temp, sums, images, texts)


def solution(mesh):
    fine = Mesh(mesh.devices.reshape(SIZES), AXES)
    rows = P(AXES, None)
    return jax.shard_map(
        local, mesh=fine, in_specs=(rows, rows, P(), P()), out_specs=(rows, rows), check_vma=False
    )
```

```python
import itertools

import jax
import jax.numpy as jnp
from jax import lax
from jax.experimental import pallas as pl
from jax.experimental.pallas import tpu as pltpu
from jax.sharding import Mesh, PartitionSpec as P

AXES = ("y", "xl", "xh", "z", "c")
SIZES = (8, 2, 2, 16, 2)

GROUP = 16

NEAR = ("xl", "xh", "c")


def moves(step):
    at = lambda x, c: x % 4 % 2 * 4 + x % 4 // 2 * 2 + c
    return [(at(x, c), at(x - step if c else x + step, 1 - c)) for x in range(4) for c in range(2)]


VMEM = pl.BlockSpec(memory_space=pltpu.VMEM)
SMEM = pl.BlockSpec(memory_space=pltpu.SMEM)


def groups():
    place = {at: n for n, at in enumerate(itertools.product(*map(range, SIZES)))}
    y, xl, xh, z, _ = map(range, SIZES)
    lines = [[place[b, i, j, k, 1] for k in z] for b in y for i in xl for j in xh]
    planes = [[place[b, i, j, k, 0] for b in y for j in xh] for i in xl for k in z]
    return lines + planes


def unit_rows(values):
    whole = values.astype(jnp.float32)
    inverse = lax.rsqrt(jnp.sum(whole * whole, axis=1, keepdims=True) + 1e-06)
    return (whole * inverse, inverse)


def back_norm(unit, inverse, grads):
    return inverse * (grads - unit * jnp.sum(unit * grads, axis=1, keepdims=True))


def unit_kernel(chip, out):
    rows = out.shape[0] // GROUP
    shard = rows // 2
    whole = chip[...].astype(jnp.float32)
    images = jnp.concatenate([whole[:shard], whole[2 * shard : 3 * shard]])
    texts = jnp.concatenate([whole[shard : 2 * shard], whole[3 * shard :]])
    half = unit_rows(jnp.where(lax.axis_index("c") == 1, images, texts))[0].astype(jnp.bfloat16)
    for k in range(GROUP):
        out[k * rows : (k + 1) * rows, :] = half


def units(chip):
    return pl.pallas_call(
        unit_kernel,
        out_shape=jax.ShapeDtypeStruct((GROUP * chip.shape[0] // 2, chip.shape[1]), jnp.bfloat16),
        in_specs=[VMEM],
        out_specs=VMEM,
        compiler_params=pltpu.CompilerParams(vmem_limit_bytes=8 << 20),
        cost_estimate=pl.CostEstimate(flops=4 * chip.size, bytes_accessed=1 << 20, transcendentals=0),
    )(chip)


def slopes(log_temp, bias, mine, got):
    scores = lax.dot_general(mine, got, (((1,), (1,)), ((), ())), preferred_element_type=jnp.float32)
    logits = jnp.exp(jnp.full((1, got.shape[0]), log_temp[0], jnp.float32)) * scores + bias[0]
    return jax.nn.sigmoid(logits)


def times(slope, got):
    return jnp.dot(slope.astype(jnp.bfloat16), got, preferred_element_type=jnp.float32)


def matching(slope, block):
    line = lax.axis_index("z") * block
    plane = (lax.axis_index("y") * SIZES[2] + lax.axis_index("xh")) * block
    image = lax.axis_index("c") == 1
    row = lax.broadcasted_iota(jnp.int32, slope.shape, 0) - jnp.where(image, line, plane)
    col = lax.broadcasted_iota(jnp.int32, slope.shape, 1) - jnp.where(image, plane, line)
    return jnp.where((row == col) & (row >= 0) & (row < block), 1.0, 0.0)


def near_kernel(log_temp, bias, mine, own, total):
    near = slopes(log_temp, bias, mine[...], own[...])
    total[...] = times(near - matching(near, mine.shape[0] // GROUP), own[...])


def far_kernel(log_temp, bias, mine, beside, above, grad):
    far = slopes(log_temp, bias, mine[...], beside[...])
    grad[...] = (above[...] + times(far, beside[...])).astype(jnp.bfloat16)


def pairs(kernel, kind, log_temp, bias, mine, got, *above):
    return pl.pallas_call(
        kernel,
        out_shape=jax.ShapeDtypeStruct(mine.shape, kind),
        in_specs=[SMEM, SMEM, VMEM, VMEM] + [VMEM] * len(above),
        out_specs=VMEM,
        compiler_params=pltpu.CompilerParams(vmem_limit_bytes=24 << 20),
        cost_estimate=pl.CostEstimate(
            flops=4 * mine.size * got.shape[0],
            bytes_accessed=3 << 20,
            transcendentals=mine.shape[0] * got.shape[0],
        ),
    )(log_temp, bias, mine, got, *above)


def end_kernel(log_temp, sums, images, texts, image_grad, text_grad):
    shard, width = images.shape
    scale = jnp.exp(jnp.full((1, width), log_temp[0], jnp.float32))
    first = pl.multiple_of(lax.axis_index("c") * shard, shard)
    text_grad[...] = back_norm(*unit_rows(texts[...]), scale * sums[pl.ds(first, shard), :])
    image_grad[...] = back_norm(*unit_rows(images[...]), scale * sums[pl.ds(first + 2 * shard, shard), :])


def end(log_temp, sums, images, texts):
    grad = jax.ShapeDtypeStruct(images.shape, jnp.float32)
    return pl.pallas_call(
        end_kernel,
        out_shape=(grad, grad),
        in_specs=[SMEM, VMEM, VMEM, VMEM],
        out_specs=(VMEM, VMEM),
        compiler_params=pltpu.CompilerParams(vmem_limit_bytes=8 << 20),
        cost_estimate=pl.CostEstimate(flops=20 * images.size, bytes_accessed=1 << 18, transcendentals=0),
    )(log_temp, sums, images, texts)


def local(images, texts, log_temp, bias):
    width = images.shape[1]
    swap = groups()

    def exchange(rows):
        parts = rows.reshape(GROUP, -1, width)
        return lax.all_to_all(parts, AXES, 0, 0, axis_index_groups=swap)

    chip = lax.all_gather(jnp.concatenate([images, texts]), "c", axis=0, tiled=True)
    mine = exchange(units(chip)).reshape(-1, width)
    beside = lax.ppermute(mine, NEAR, moves(1))
    own = jnp.concatenate([lax.ppermute(half, NEAR, moves(0)) for half in jnp.split(mine, 2)])
    total = pairs(near_kernel, jnp.float32, log_temp, bias, mine, own)
    grad = pairs(far_kernel, jnp.bfloat16, log_temp, bias, mine, beside, total)
    share = jnp.sum(exchange(grad).astype(jnp.float32), axis=0)
    sums = lax.all_gather(share, "c", axis=0, tiled=True)
    return end(log_temp, sums, images, texts)


def solution(mesh):
    fine = Mesh(mesh.devices.reshape(SIZES), AXES)
    rows = P(AXES, None)
    return jax.shard_map(
        local, mesh=fine, in_specs=(rows, rows, P(), P()), out_specs=(rows, rows), check_vma=False
    )
```

```python
import itertools

import jax
import jax.numpy as jnp
from jax import lax
from jax.experimental import pallas as pl
from jax.experimental.pallas import tpu as pltpu
from jax.sharding import Mesh, PartitionSpec as P

AXES = ("y", "xl", "xh", "z", "c")
SIZES = (8, 2, 2, 16, 2)

GROUP = 16
HALF = GROUP // 2

NEAR = ("xl", "xh", "c")


def moves(step):
    at = lambda x, c: x % 4 % 2 * 4 + x % 4 // 2 * 2 + c
    return [(at(x, c), at(x - step if c else x + step, 1 - c)) for x in range(4) for c in range(2)]


VMEM = pl.BlockSpec(memory_space=pltpu.VMEM)
SMEM = pl.BlockSpec(memory_space=pltpu.SMEM)


def halves():
    place = {at: n for n, at in enumerate(itertools.product(*map(range, SIZES)))}
    y, xl, xh, z, _ = map(range, SIZES)
    lines = [[place[b, i, j, k, 1] for k in z[odd::2]] for b in y for i in xl for j in xh for odd in range(2)]
    planes = [[place[b, i, j, k, 0] for b in y[odd::2] for j in xh] for i in xl for k in z for odd in range(2)]
    return lines + planes


def groups():
    parts = halves()
    return [even + odd for even, odd in zip(parts[::2], parts[1::2])]


PAIR = ("y", "z", "c")
SWAP = [
    ((y * SIZES[3] + z) * 2 + c, ((y if c else y ^ 1) * SIZES[3] + (z ^ 1 if c else z)) * 2 + c)
    for y in range(SIZES[0])
    for z in range(SIZES[3])
    for c in range(2)
]


def unit_rows(values):
    whole = values.astype(jnp.float32)
    inverse = lax.rsqrt(jnp.sum(whole * whole, axis=1, keepdims=True) + 1e-06)
    return (whole * inverse, inverse)


def back_norm(unit, inverse, grads):
    return inverse * (grads - unit * jnp.sum(unit * grads, axis=1, keepdims=True))


def unit_kernel(chip, out):
    rows = out.shape[0] // HALF
    shard = rows // 2
    whole = chip[...].astype(jnp.float32)
    images = jnp.concatenate([whole[:shard], whole[2 * shard : 3 * shard]])
    texts = jnp.concatenate([whole[shard : 2 * shard], whole[3 * shard :]])
    half = unit_rows(jnp.where(lax.axis_index("c") == 1, images, texts))[0].astype(jnp.bfloat16)
    for k in range(HALF):
        out[k * rows : (k + 1) * rows, :] = half


def units(chip):
    return pl.pallas_call(
        unit_kernel,
        out_shape=jax.ShapeDtypeStruct((HALF * chip.shape[0] // 2, chip.shape[1]), jnp.bfloat16),
        in_specs=[VMEM],
        out_specs=VMEM,
        compiler_params=pltpu.CompilerParams(vmem_limit_bytes=8 << 20),
        cost_estimate=pl.CostEstimate(flops=4 * chip.size, bytes_accessed=1 << 20, transcendentals=0),
    )(chip)


def pairs_kernel(log_temp, bias, mine, swapped, first, second, beside, grad):
    half = mine.shape[0]
    block = half // HALF
    y, z = lax.axis_index("y"), lax.axis_index("z")
    line, plane = z // 2 * block, (y // 2 * SIZES[2] + lax.axis_index("xh")) * block
    image = lax.axis_index("c") == 1
    rows = jnp.concatenate([mine[...], swapped[...]])
    total = jnp.zeros(rows.shape, jnp.float32)
    for got in (first, second, beside):
        scores = lax.dot_general(
            rows, got[...], (((1,), (1,)), ((), ())), preferred_element_type=jnp.float32
        )
        logits = jnp.exp(jnp.full((1, got.shape[0]), log_temp[0], jnp.float32)) * scores + bias[0]
        slope = jax.nn.sigmoid(logits)
        if got is first:
            row = lax.broadcasted_iota(jnp.int32, slope.shape, 0) - jnp.where(image, line, plane)
            col = lax.broadcasted_iota(jnp.int32, slope.shape, 1) - jnp.where(image, plane, line)
            same = (row == col) & (row >= 0) & (row < block)
            slope = slope - jnp.where(same, 1.0, 0.0)
        total = total + jnp.dot(slope.astype(jnp.bfloat16), got[...], preferred_element_type=jnp.float32)
    odd = lax.rem(jnp.where(image, z, y), 2)
    grad[pl.ds(pl.multiple_of(odd * half, half), half), :] = total[:half].astype(jnp.bfloat16)
    grad[pl.ds(pl.multiple_of((1 - odd) * half, half), half), :] = total[half:].astype(jnp.bfloat16)


def pairs(log_temp, bias, mine, swapped, first, second, beside):
    rows, width = 2 * mine.shape[0], mine.shape[1]
    return pl.pallas_call(
        pairs_kernel,
        out_shape=jax.ShapeDtypeStruct((rows, width), jnp.bfloat16),
        in_specs=[SMEM, SMEM] + [VMEM] * 5,
        out_specs=VMEM,
        compiler_params=pltpu.CompilerParams(vmem_limit_bytes=24 << 20),
        cost_estimate=pl.CostEstimate(
            flops=8 * rows * rows * width, bytes_accessed=3 << 20, transcendentals=2 * rows * rows
        ),
    )(log_temp, bias, mine, swapped, first, second, beside)


def end_kernel(log_temp, sums, images, texts, image_grad, text_grad):
    shard, width = images.shape
    scale = jnp.exp(jnp.full((1, width), log_temp[0], jnp.float32))
    first = pl.multiple_of(lax.axis_index("c") * shard, shard)
    text_grad[...] = back_norm(*unit_rows(texts[...]), scale * sums[pl.ds(first, shard), :])
    image_grad[...] = back_norm(*unit_rows(images[...]), scale * sums[pl.ds(first + 2 * shard, shard), :])


def end(log_temp, sums, images, texts):
    grad = jax.ShapeDtypeStruct(images.shape, jnp.float32)
    return pl.pallas_call(
        end_kernel,
        out_shape=(grad, grad),
        in_specs=[SMEM, VMEM, VMEM, VMEM],
        out_specs=(VMEM, VMEM),
        compiler_params=pltpu.CompilerParams(vmem_limit_bytes=8 << 20),
        cost_estimate=pl.CostEstimate(flops=20 * images.size, bytes_accessed=1 << 18, transcendentals=0),
    )(log_temp, sums, images, texts)


def local(images, texts, log_temp, bias):
    width = images.shape[1]

    def exchange(rows, among):
        parts = rows.reshape(len(among[0]), -1, width)
        return lax.all_to_all(parts, AXES, 0, 0, axis_index_groups=among)

    chip = lax.all_gather(jnp.concatenate([images, texts]), "c", axis=0, tiled=True)
    mine = exchange(units(chip), halves()).reshape(-1, width)
    swapped = lax.ppermute(mine, PAIR, SWAP)
    beside = jnp.concatenate([lax.ppermute(rows, NEAR, moves(1)) for rows in (mine, swapped)])
    own = [lax.ppermute(rows, NEAR, moves(0)) for rows in (mine, swapped)]
    grad = pairs(log_temp, bias, mine, swapped, *own, beside)
    share = jnp.sum(exchange(grad, groups()).astype(jnp.float32), axis=0)
    sums = lax.all_gather(share, "c", axis=0, tiled=True)
    return end(log_temp, sums, images, texts)


def solution(mesh):
    fine = Mesh(mesh.devices.reshape(SIZES), AXES)
    rows = P(AXES, None)
    return jax.shard_map(
        local, mesh=fine, in_specs=(rows, rows, P(), P()), out_specs=(rows, rows), check_vma=False
    )
```

```python
import itertools

import jax
import jax.numpy as jnp
from jax import lax
from jax.experimental import pallas as pl
from jax.experimental.pallas import tpu as pltpu
from jax.sharding import Mesh, PartitionSpec as P

AXES = ("y", "xl", "xh", "z", "c")
SIZES = (8, 2, 2, 16, 2)

GROUP = 16
HALF = GROUP // 2

NEAR = ("xl", "xh", "c")


def moves(step):
    at = lambda x, c: x % 4 % 2 * 4 + x % 4 // 2 * 2 + c
    return [(at(x, c), at(x - step if c else x + step, 1 - c)) for x in range(4) for c in range(2)]


VMEM = pl.BlockSpec(memory_space=pltpu.VMEM)
SMEM = pl.BlockSpec(memory_space=pltpu.SMEM)


def halves():
    place = {at: n for n, at in enumerate(itertools.product(*map(range, SIZES)))}
    y, xl, xh, z, _ = map(range, SIZES)
    lines = [[place[b, i, j, k, 1] for k in z[odd::2]] for b in y for i in xl for j in xh for odd in range(2)]
    planes = [[place[b, i, j, k, 0] for b in y[odd::2] for j in xh] for i in xl for k in z for odd in range(2)]
    return lines + planes


def groups():
    parts = halves()
    return [[n for pair in zip(even, odd) for n in pair] for even, odd in zip(parts[::2], parts[1::2])]


PAIR = ("y", "z", "c")
SWAP = [
    ((y * SIZES[3] + z) * 2 + c, ((y if c else y ^ 1) * SIZES[3] + (z ^ 1 if c else z)) * 2 + c)
    for y in range(SIZES[0])
    for z in range(SIZES[3])
    for c in range(2)
]


def unit_rows(values):
    whole = values.astype(jnp.float32)
    inverse = lax.rsqrt(jnp.sum(whole * whole, axis=1, keepdims=True) + 1e-06)
    return (whole * inverse, inverse)


def back_norm(unit, inverse, grads):
    return inverse * (grads - unit * jnp.sum(unit * grads, axis=1, keepdims=True))


def unit_kernel(chip, out):
    rows = out.shape[0] // HALF
    shard = rows // 2
    whole = chip[...].astype(jnp.float32)
    images = jnp.concatenate([whole[:shard], whole[2 * shard : 3 * shard]])
    texts = jnp.concatenate([whole[shard : 2 * shard], whole[3 * shard :]])
    half = unit_rows(jnp.where(lax.axis_index("c") == 1, images, texts))[0].astype(jnp.bfloat16)
    for k in range(HALF):
        out[k * rows : (k + 1) * rows, :] = half


def units(chip):
    return pl.pallas_call(
        unit_kernel,
        out_shape=jax.ShapeDtypeStruct((HALF * chip.shape[0] // 2, chip.shape[1]), jnp.bfloat16),
        in_specs=[VMEM],
        out_specs=VMEM,
        compiler_params=pltpu.CompilerParams(vmem_limit_bytes=8 << 20),
        cost_estimate=pl.CostEstimate(flops=4 * chip.size, bytes_accessed=1 << 20, transcendentals=0),
    )(chip)


def pairs_kernel(log_temp, bias, mine, swapped, first, second, beside, grad):
    half = mine.shape[0]
    block = half // HALF
    y, z = lax.axis_index("y"), lax.axis_index("z")
    line, plane = z // 2 * block, (y // 2 * SIZES[2] + lax.axis_index("xh")) * block
    image = lax.axis_index("c") == 1
    rows = jnp.concatenate([mine[...], swapped[...]])
    total = jnp.zeros(rows.shape, jnp.float32)
    for got in (first, second, beside):
        scores = lax.dot_general(
            rows, got[...], (((1,), (1,)), ((), ())), preferred_element_type=jnp.float32
        )
        logits = jnp.exp(jnp.full((1, got.shape[0]), log_temp[0], jnp.float32)) * scores + bias[0]
        slope = jax.nn.sigmoid(logits)
        if got is first:
            row = lax.broadcasted_iota(jnp.int32, slope.shape, 0) - jnp.where(image, line, plane)
            col = lax.broadcasted_iota(jnp.int32, slope.shape, 1) - jnp.where(image, plane, line)
            same = (row == col) & (row >= 0) & (row < block)
            slope = slope - jnp.where(same, 1.0, 0.0)
        total = total + jnp.dot(slope.astype(jnp.bfloat16), got[...], preferred_element_type=jnp.float32)
    odd = lax.rem(jnp.where(image, z, y), 2)
    for k in range(GROUP):
        place = 2 * (k % HALF) + (odd if k < HALF else 1 - odd)
        part = total[k * block : (k + 1) * block].astype(jnp.bfloat16)
        grad[pl.ds(pl.multiple_of(place * block, block), block), :] = part


def pairs(log_temp, bias, mine, swapped, first, second, beside):
    rows, width = 2 * mine.shape[0], mine.shape[1]
    return pl.pallas_call(
        pairs_kernel,
        out_shape=jax.ShapeDtypeStruct((rows, width), jnp.bfloat16),
        in_specs=[SMEM, SMEM] + [VMEM] * 5,
        out_specs=VMEM,
        compiler_params=pltpu.CompilerParams(vmem_limit_bytes=24 << 20),
        cost_estimate=pl.CostEstimate(
            flops=8 * rows * rows * width, bytes_accessed=3 << 20, transcendentals=2 * rows * rows
        ),
    )(log_temp, bias, mine, swapped, first, second, beside)


def end_kernel(log_temp, sums, images, texts, image_grad, text_grad):
    shard, width = images.shape
    scale = jnp.exp(jnp.full((1, width), log_temp[0], jnp.float32))
    first = pl.multiple_of(lax.axis_index("c") * shard, shard)
    text_grad[...] = back_norm(*unit_rows(texts[...]), scale * sums[pl.ds(first, shard), :])
    image_grad[...] = back_norm(*unit_rows(images[...]), scale * sums[pl.ds(first + 2 * shard, shard), :])


def end(log_temp, sums, images, texts):
    grad = jax.ShapeDtypeStruct(images.shape, jnp.float32)
    return pl.pallas_call(
        end_kernel,
        out_shape=(grad, grad),
        in_specs=[SMEM, VMEM, VMEM, VMEM],
        out_specs=(VMEM, VMEM),
        compiler_params=pltpu.CompilerParams(vmem_limit_bytes=8 << 20),
        cost_estimate=pl.CostEstimate(flops=20 * images.size, bytes_accessed=1 << 18, transcendentals=0),
    )(log_temp, sums, images, texts)


def local(images, texts, log_temp, bias):
    width = images.shape[1]

    def exchange(rows, among):
        parts = rows.reshape(len(among[0]), -1, width)
        return lax.all_to_all(parts, AXES, 0, 0, axis_index_groups=among)

    chip = lax.all_gather(jnp.concatenate([images, texts]), "c", axis=0, tiled=True)
    mine = exchange(units(chip), halves()).reshape(-1, width)
    swapped = lax.ppermute(mine, PAIR, SWAP)
    beside = jnp.concatenate([lax.ppermute(rows, NEAR, moves(1)) for rows in (mine, swapped)])
    own = [lax.ppermute(rows, NEAR, moves(0)) for rows in (mine, swapped)]
    grad = pairs(log_temp, bias, mine, swapped, *own, beside)
    share = jnp.sum(exchange(grad, groups()).astype(jnp.float32), axis=0)
    sums = lax.all_gather(share, "c", axis=0, tiled=True)
    return end(log_temp, sums, images, texts)


def solution(mesh):
    fine = Mesh(mesh.devices.reshape(SIZES), AXES)
    rows = P(AXES, None)
    return jax.shard_map(
        local, mesh=fine, in_specs=(rows, rows, P(), P()), out_specs=(rows, rows), check_vma=False
    )
```

```python
import itertools

import jax
import jax.numpy as jnp
from jax import lax
from jax.experimental import pallas as pl
from jax.experimental.pallas import tpu as pltpu
from jax.sharding import Mesh, PartitionSpec as P

AXES = ("y", "xl", "xh", "z", "c")
SIZES = (8, 2, 2, 16, 2)

GROUP = 16

NEAR = ("xl", "xh", "c")


def moves(step):
    at = lambda x, c: x % 4 % 2 * 4 + x % 4 // 2 * 2 + c
    return [(at(x, c), at(x - step if c else x + step, 1 - c)) for x in range(4) for c in range(2)]


VMEM = pl.BlockSpec(memory_space=pltpu.VMEM)
SMEM = pl.BlockSpec(memory_space=pltpu.SMEM)


def groups():
    place = {at: n for n, at in enumerate(itertools.product(*map(range, SIZES)))}
    y, xl, xh, z, _ = map(range, SIZES)
    lines = [[place[b, i, j, k, 1] for k in z] for b in y for i in xl for j in xh]
    planes = [[place[b, i, j, k, 0] for b in y for j in xh] for i in xl for k in z]
    return lines + planes


def unit_rows(values):
    whole = values.astype(jnp.float32)
    inverse = lax.rsqrt(jnp.sum(whole * whole, axis=1, keepdims=True) + 1e-06)
    return (whole * inverse, inverse)


def back_norm(unit, inverse, grads):
    return inverse * (grads - unit * jnp.sum(unit * grads, axis=1, keepdims=True))


def unit_kernel(chip, out):
    rows = out.shape[0] // GROUP
    shard = rows // 2
    whole = chip[...].astype(jnp.float32)
    images = jnp.concatenate([whole[:shard], whole[2 * shard : 3 * shard]])
    texts = jnp.concatenate([whole[shard : 2 * shard], whole[3 * shard :]])
    half = unit_rows(jnp.where(lax.axis_index("c") == 1, images, texts))[0].astype(jnp.bfloat16)
    for k in range(GROUP):
        out[k * rows : (k + 1) * rows, :] = half


def units(chip):
    return pl.pallas_call(
        unit_kernel,
        out_shape=jax.ShapeDtypeStruct((GROUP * chip.shape[0] // 2, chip.shape[1]), jnp.bfloat16),
        in_specs=[VMEM],
        out_specs=VMEM,
        compiler_params=pltpu.CompilerParams(vmem_limit_bytes=8 << 20),
        cost_estimate=pl.CostEstimate(flops=4 * chip.size, bytes_accessed=1 << 20, transcendentals=0),
    )(chip)


def pairs_kernel(log_temp, bias, mine, first, second, beside, grad):
    block = mine.shape[0] // GROUP
    line = lax.axis_index("z") * block
    plane = (lax.axis_index("y") * SIZES[2] + lax.axis_index("xh")) * block
    image = lax.axis_index("c") == 1
    total = jnp.zeros(mine.shape, jnp.float32)
    for got, start in ((first, 0), (second, first.shape[0]), (beside, None)):
        scores = lax.dot_general(
            mine[...], got[...], (((1,), (1,)), ((), ())), preferred_element_type=jnp.float32
        )
        logits = jnp.exp(jnp.full((1, got.shape[0]), log_temp[0], jnp.float32)) * scores + bias[0]
        slope = jax.nn.sigmoid(logits)
        if start is not None:
            row = lax.broadcasted_iota(jnp.int32, slope.shape, 0) - jnp.where(image, line, plane)
            col = lax.broadcasted_iota(jnp.int32, slope.shape, 1) + start - jnp.where(image, plane, line)
            same = (row == col) & (row >= 0) & (row < block)
            slope = slope - jnp.where(same, 1.0, 0.0)
        total = total + jnp.dot(slope.astype(jnp.bfloat16), got[...], preferred_element_type=jnp.float32)
    grad[...] = total.astype(jnp.bfloat16)


def pairs(log_temp, bias, mine, first, second, beside):
    others = first.shape[0] + second.shape[0] + beside.shape[0]
    return pl.pallas_call(
        pairs_kernel,
        out_shape=jax.ShapeDtypeStruct(mine.shape, jnp.bfloat16),
        in_specs=[SMEM, SMEM, VMEM, VMEM, VMEM, VMEM],
        out_specs=VMEM,
        compiler_params=pltpu.CompilerParams(vmem_limit_bytes=24 << 20),
        cost_estimate=pl.CostEstimate(
            flops=4 * mine.size * others, bytes_accessed=3 << 20, transcendentals=mine.shape[0] * others
        ),
    )(log_temp, bias, mine, first, second, beside)


def end_kernel(log_temp, sums, images, texts, image_grad, text_grad):
    shard, width = images.shape
    scale = jnp.exp(jnp.full((1, width), log_temp[0], jnp.float32))
    first = pl.multiple_of(lax.axis_index("c") * shard, shard)
    text_grad[...] = back_norm(*unit_rows(texts[...]), scale * sums[pl.ds(first, shard), :])
    image_grad[...] = back_norm(*unit_rows(images[...]), scale * sums[pl.ds(first + 2 * shard, shard), :])


def end(log_temp, sums, images, texts):
    grad = jax.ShapeDtypeStruct(images.shape, jnp.float32)
    return pl.pallas_call(
        end_kernel,
        out_shape=(grad, grad),
        in_specs=[SMEM, VMEM, VMEM, VMEM],
        out_specs=(VMEM, VMEM),
        compiler_params=pltpu.CompilerParams(vmem_limit_bytes=8 << 20),
        cost_estimate=pl.CostEstimate(flops=20 * images.size, bytes_accessed=1 << 18, transcendentals=0),
    )(log_temp, sums, images, texts)


def local(images, texts, log_temp, bias):
    width = images.shape[1]
    swap = groups()

    def exchange(rows):
        parts = rows.reshape(GROUP, -1, width)
        return lax.all_to_all(parts, AXES, 0, 0, axis_index_groups=swap)

    chip = lax.all_gather(jnp.concatenate([images, texts]), "c", axis=0, tiled=True)
    mine = exchange(units(chip)).reshape(-1, width)
    parts = zip(jnp.split(mine, 2), (1, -1))
    beside = jnp.concatenate([lax.ppermute(half, NEAR, moves(step)) for half, step in parts])
    own = [lax.ppermute(half, NEAR, moves(0)) for half in jnp.split(mine, 2)]
    grad = pairs(log_temp, bias, mine, *own, beside)
    share = jnp.sum(exchange(grad).astype(jnp.float32), axis=0)
    sums = lax.all_gather(share, "c", axis=0, tiled=True)
    return end(log_temp, sums, images, texts)


def solution(mesh):
    fine = Mesh(mesh.devices.reshape(SIZES), AXES)
    rows = P(AXES, None)
    return jax.shard_map(
        local, mesh=fine, in_specs=(rows, rows, P(), P()), out_specs=(rows, rows), check_vma=False
    )
```

```python
import itertools

import jax
import jax.numpy as jnp
from jax import lax
from jax.experimental import pallas as pl
from jax.experimental.pallas import tpu as pltpu
from jax.sharding import Mesh, PartitionSpec as P

AXES = ("y", "xl", "xh", "z", "c")
SIZES = (8, 2, 2, 16, 2)

GROUP = 16

NEAR = ("xl", "xh", "c")


def moves(step):
    at = lambda x, c: x % 4 % 2 * 4 + x % 4 // 2 * 2 + c
    return [(at(x, c), at(x - step if c else x + step, 1 - c)) for x in range(4) for c in range(2)]


VMEM = pl.BlockSpec(memory_space=pltpu.VMEM)


def groups():
    place = {at: n for n, at in enumerate(itertools.product(*map(range, SIZES)))}
    y, xl, xh, z, _ = map(range, SIZES)
    lines = [[place[b, i, j, k, 1] for k in z] for b in y for i in xl for j in xh]
    planes = [[place[b, i, j, k, 0] for b in y for j in xh] for i in xl for k in z]
    return lines + planes


def unit_rows(values):
    whole = values.astype(jnp.float32)
    inverse = lax.rsqrt(jnp.sum(whole * whole, axis=1, keepdims=True) + 1e-06)
    return (whole * inverse, inverse)


def back_norm(unit, inverse, grads):
    return inverse * (grads - unit * jnp.sum(unit * grads, axis=1, keepdims=True))


def unit_kernel(chip, out):
    rows = out.shape[0] // GROUP
    shard = rows // 2
    whole = chip[...].astype(jnp.float32)
    images = jnp.concatenate([whole[:shard], whole[2 * shard : 3 * shard]])
    texts = jnp.concatenate([whole[shard : 2 * shard], whole[3 * shard :]])
    half = unit_rows(jnp.where(lax.axis_index("c") == 1, images, texts))[0].astype(jnp.bfloat16)
    for k in range(GROUP):
        out[k * rows : (k + 1) * rows, :] = half


def units(chip):
    return pl.pallas_call(
        unit_kernel,
        out_shape=jax.ShapeDtypeStruct((GROUP * chip.shape[0] // 2, chip.shape[1]), jnp.bfloat16),
        in_specs=[VMEM],
        out_specs=VMEM,
        compiler_params=pltpu.CompilerParams(vmem_limit_bytes=8 << 20),
        cost_estimate=pl.CostEstimate(flops=4 * chip.size, bytes_accessed=1 << 20, transcendentals=0),
    )(chip)


def pairs_kernel(log_temp, bias, mine, first, second, beside, grad):
    block = mine.shape[0] // GROUP
    line = lax.axis_index("z") * block
    plane = (lax.axis_index("y") * SIZES[2] + lax.axis_index("xh")) * block
    image = lax.axis_index("c") == 1
    total = jnp.zeros(mine.shape, jnp.float32)
    for got, start in ((first, 0), (second, first.shape[0]), (beside, None)):
        scores = lax.dot_general(
            mine[...], got[...], (((1,), (1,)), ((), ())), preferred_element_type=jnp.float32
        )
        logits = jnp.exp(log_temp[...]) * scores + bias[...]
        slope = jax.nn.sigmoid(logits)
        if start is not None:
            row = lax.broadcasted_iota(jnp.int32, slope.shape, 0) - jnp.where(image, line, plane)
            col = lax.broadcasted_iota(jnp.int32, slope.shape, 1) + start - jnp.where(image, plane, line)
            same = (row == col) & (row >= 0) & (row < block)
            slope = slope - jnp.where(same, 1.0, 0.0)
        total = total + jnp.dot(slope.astype(jnp.bfloat16), got[...], preferred_element_type=jnp.float32)
    grad[...] = total.astype(jnp.bfloat16)


def pairs(log_temp, bias, mine, first, second, beside):
    others = first.shape[0] + second.shape[0] + beside.shape[0]
    return pl.pallas_call(
        pairs_kernel,
        out_shape=jax.ShapeDtypeStruct(mine.shape, jnp.bfloat16),
        in_specs=[VMEM, VMEM, VMEM, VMEM, VMEM, VMEM],
        out_specs=VMEM,
        compiler_params=pltpu.CompilerParams(vmem_limit_bytes=24 << 20),
        cost_estimate=pl.CostEstimate(
            flops=4 * mine.size * others, bytes_accessed=3 << 20, transcendentals=mine.shape[0] * others
        ),
    )(log_temp, bias, mine, first, second, beside)


def end_kernel(log_temp, sums, images, texts, image_grad, text_grad):
    shard = images.shape[0]
    scale = jnp.exp(log_temp[...])
    first = pl.multiple_of(lax.axis_index("c") * shard, shard)
    text_grad[...] = back_norm(*unit_rows(texts[...]), scale * sums[pl.ds(first, shard), :])
    image_grad[...] = back_norm(*unit_rows(images[...]), scale * sums[pl.ds(first + 2 * shard, shard), :])


def end(log_temp, sums, images, texts):
    grad = jax.ShapeDtypeStruct(images.shape, jnp.float32)
    return pl.pallas_call(
        end_kernel,
        out_shape=(grad, grad),
        in_specs=[VMEM, VMEM, VMEM, VMEM],
        out_specs=(VMEM, VMEM),
        compiler_params=pltpu.CompilerParams(vmem_limit_bytes=8 << 20),
        cost_estimate=pl.CostEstimate(flops=20 * images.size, bytes_accessed=1 << 18, transcendentals=0),
    )(log_temp, sums, images, texts)


def local(images, texts, log_temp, bias):
    width = images.shape[1]
    log_temp, bias = log_temp.reshape(1, 1), bias.reshape(1, 1)
    swap = groups()

    def exchange(rows):
        parts = rows.reshape(GROUP, -1, width)
        return lax.all_to_all(parts, AXES, 0, 0, axis_index_groups=swap)

    chip = lax.all_gather(jnp.concatenate([images, texts]), "c", axis=0, tiled=True)
    mine = exchange(units(chip)).reshape(-1, width)
    parts = zip(jnp.split(mine, 2), (1, -1))
    beside = jnp.concatenate([lax.ppermute(half, NEAR, moves(step)) for half, step in parts])
    own = [lax.ppermute(half, NEAR, moves(0)) for half in jnp.split(mine, 2)]
    grad = pairs(log_temp, bias, mine, *own, beside)
    share = jnp.sum(exchange(grad).astype(jnp.float32), axis=0)
    sums = lax.all_gather(share, "c", axis=0, tiled=True)
    return end(log_temp, sums, images, texts)


def solution(mesh):
    fine = Mesh(mesh.devices.reshape(SIZES), AXES)
    rows = P(AXES, None)
    return jax.shard_map(
        local, mesh=fine, in_specs=(rows, rows, P(), P()), out_specs=(rows, rows), check_vma=False
    )
```
